32 devices in a mesh: gx: 4 (over y, x), gy: 8 (over z, core).
Axes of the slice: x: 2, y: 2, z: 4, core: 2. Of those that a mesh axis runs over, the one named last changes fastest.
Arguments:
- features: bfloat16 [16, 128, 128, 128], P(None, 'gx', 'gy'), may hold values from -24 to 24
- w_first: bfloat16 [27, 16, 16], replicated, may hold values from -0.3125 to 0.3125
- w_second: bfloat16 [27, 16, 16], replicated, may hold values from -0.3125 to 0.3125
- w_lift: bfloat16 [512, 16], replicated, may hold values from -1.5 to 1.5
- w_coarse: bfloat16 [512, 27, 512], P('gy'), may hold values from -0.0546875 to 0.0546875
- w_decode: bfloat16 [16, 512], replicated, may hold values from -0.25 to 0.25
- w_joining: bfloat16 [16, 32], replicated, may hold values from -1 to 1
Outputs:
- joined: bfloat16 [16, 128, 128, 128], P(None, 'gx', 'gy')
The draws below stay inside these ranges and needn't reach their ends.
All inputs are finite; a program needn't handle non-finite values.
Results may differ from the reference program's by a relative error of at most 0.0065.
Values may be sent and summed in bfloat16 or wider, within the bound.
A program may use at most 192 MiB of HBM per device.

```python
import math
import jax
import jax.numpy as jnp

C = 16
CC = 512
POOL = 16
NZ = 128
NX = 128
NY = 128


def draw_features(key, part):
    key_scale, key_offset, key_noise = jax.random.split(jax.random.fold_in(key, 11), 3)
    blocks = (C, NX // POOL, NY // POOL, NZ // POOL)
    scale = jnp.exp(jax.random.uniform(key_scale, blocks, jnp.float32, math.log(0.3), math.log(3.0)))
    offset = 0.7 * jax.random.normal(key_offset, blocks, jnp.float32)
    noise = jax.random.normal(key_noise, (C, NX, NY, NZ), jnp.float32)

    def spread(small):
        return jnp.repeat(jnp.repeat(jnp.repeat(small, POOL, 1), POOL, 2), POOL, 3)
    return jnp.clip((noise + spread(offset)) * spread(scale), -24.0, 24.0).astype(jnp.bfloat16)


def block_levels(key, dims, pieces, smallest, top_value):
    def one(axis_at, blocks):
        draws = jax.random.uniform(jax.random.fold_in(jax.random.fold_in(key, 6), axis_at), (blocks,), jnp.float32, smallest / len(pieces), top_value / len(pieces))
        return jnp.repeat(jnp.exp(draws), dims[axis_at] // blocks).reshape((-1,) + (1,) * (len(dims) - axis_at - 1))

    factor_of = one(*pieces[0])
    for cut in pieces[1:]:
        factor_of = factor_of * one(*cut)
    return factor_of


def normal_values(rng, extent, deviation, most, shards=(), kind=jnp.bfloat16):
    drawn = deviation * jax.random.normal(rng, extent, jnp.float32)
    if shards:
        drawn = drawn * block_levels(rng, extent, shards, -0.22, 0.18)
    return jnp.clip(drawn, -most, most).astype(kind)


def setup_inputs(seed: int = 0) -> dict:
    key_list = jax.random.split(jax.random.key(seed), 8)
    features = draw_features(jax.random.fold_in(key_list[7], 71), 0)
    w_first = normal_values(key_list[1], (27, C, C), (27 * C) ** -0.5, 0.3125)
    w_second = normal_values(key_list[2], (27, C, C), (27 * C) ** -0.5, 0.3125)
    w_lift = normal_values(key_list[3], (CC, C), C ** -0.5, 1.5)
    w_coarse = normal_values(key_list[4], (CC, 27, CC), (27 * CC) ** -0.5, 0.0546875, ((0, 8),))
    w_decode = normal_values(key_list[5], (C, CC), CC ** -0.5, 0.25)
    w_joining = normal_values(key_list[6], (C, 2 * C), (2 * C) ** -0.5, 1.0)
    return {"features": features, "w_first": w_first, "w_second": w_second, "w_lift": w_lift, "w_coarse": w_coarse, "w_decode": w_decode, "w_joining": w_joining}


def conv_full(field, weight):
    count = weight.shape[1]
    padded = jnp.pad(field.astype(jnp.float32), ((0, 0), (1, 1), (1, 1), (1, 1)))
    size_x, size_y, size_z = field.shape[1], field.shape[2], field.shape[3]
    total = jnp.zeros((count, size_x, size_y, size_z), jnp.float32)
    for offset in range(27):
        shift_a, shift_b, shift_c = offset // 9, (offset // 3) % 3, offset % 3
        window = padded[:, shift_a:shift_a + size_x, shift_b:shift_b + size_y, shift_c:shift_c + size_z]
        total = total + jnp.einsum("oc,cxyz->oxyz", weight[offset].astype(jnp.float32), window)
    return total


def reference(features, w_first, w_second, w_lift, w_coarse, w_decode, w_joining):
    first = jnp.maximum(conv_full(features, w_first), 0.0).astype(jnp.bfloat16)
    second = jnp.maximum(conv_full(first, w_second), 0.0).astype(jnp.bfloat16)
    blocks = second.astype(jnp.float32).reshape(C, NX // POOL, POOL, NY // POOL, POOL, NZ // POOL, POOL)
    pooled = jnp.mean(blocks, axis=(2, 4, 6))
    lifted = jnp.maximum(jnp.einsum("oc,cxyz->oxyz", w_lift.astype(jnp.float32), pooled), 0.0).astype(jnp.bfloat16)
    coarse = jnp.maximum(conv_full(lifted, jnp.transpose(w_coarse, (1, 0, 2))), 0.0).astype(jnp.bfloat16)
    decoded = jnp.einsum("oc,cxyz->oxyz", w_decode.astype(jnp.float32), coarse.astype(jnp.float32)).astype(jnp.bfloat16)
    upsampled = jnp.repeat(jnp.repeat(jnp.repeat(decoded, POOL, 1), POOL, 2), POOL, 3)
    joined = jnp.einsum("oc,cxyz->oxyz", w_joining[:, :C].astype(jnp.float32), second.astype(jnp.float32))
    joined = joined + jnp.einsum("oc,cxyz->oxyz", w_joining[:, C:].astype(jnp.float32), upsampled.astype(jnp.float32))
    return joined.astype(jnp.bfloat16)
```

```python
import jax
import jax.numpy as jnp
import numpy as np
from jax import lax
from jax.experimental import pallas as pl
from jax.experimental.pallas import tpu as pltpu
from jax.sharding import PartitionSpec as P

POOL = 16
FAR = 4096
VMEM_LIMIT = 48 * 1024 * 1024


def rows_of(chans, size_y, width):
    own_c = np.repeat(np.arange(chans), size_y)
    own_y = np.tile(np.arange(size_y), chans)
    side_y = list(range(-width, 0)) + list(range(size_y, size_y + width))
    rim_c = np.tile(np.arange(chans), len(side_y))
    rim_y = np.repeat(np.array(side_y, dtype=np.int64), chans)
    return np.concatenate([own_c, rim_c]), np.concatenate([own_y, rim_y])


def spread_maps(chans, size_y, out_width, in_width):
    out_c, out_y = rows_of(chans, size_y, out_width)
    in_c, in_y = rows_of(chans, size_y, in_width)
    rows, cols = len(out_c), len(in_c)
    left = np.zeros((3 * rows, 3 * chans), np.float32)
    right = np.zeros((3 * chans, 3 * cols), np.float32)
    for tap in range(3):
        left[tap * rows + np.arange(rows), tap * chans + out_c] = 1.0
        right[tap * chans + in_c, tap * cols + np.arange(cols)] = 1.0
    as_bf = lambda v: jnp.asarray(v, jnp.bfloat16)
    return (
        as_bf(left),
        as_bf(right),
        jnp.asarray(np.tile(out_y, 3)[:, None], jnp.int32),
        jnp.asarray(np.tile(in_y, 3)[None, :], jnp.int32),
    )


def build_matrix(weight_ref, left_ref, right_ref, out_y_ref, in_y_ref, matrix_ref):
    gap = in_y_ref[...] - out_y_ref[...]
    total = jnp.zeros(matrix_ref.shape, jnp.float32)
    for shift_b in range(3):
        part = jnp.dot(left_ref[...], weight_ref[shift_b], preferred_element_type=jnp.float32)
        part = jnp.dot(
            part.astype(jnp.bfloat16), right_ref[...], preferred_element_type=jnp.float32
        )
        total = jnp.where(gap == shift_b - 1, part, total)
    matrix_ref[...] = total.astype(jnp.bfloat16)


def shift_sum(parts, rows, group, depth):
    lane = lax.broadcasted_iota(jnp.int32, (rows, depth), 1)
    planes = []
    for plane in range(group):
        cut = parts[:, plane * depth : (plane + 1) * depth]
        before = jnp.where(lane == 0, 0.0, pltpu.roll(cut[:rows], 1, 1))
        after = jnp.where(lane == depth - 1, 0.0, pltpu.roll(cut[2 * rows :], depth - 1, 1))
        planes.append(before + cut[rows : 2 * rows] + after)
    return planes


def stack_planes(planes, group):
    return jnp.concatenate(
        [jnp.concatenate(planes[a : a + group], axis=1) for a in range(3)], axis=0
    )


def fine_kernel(
    own_ref, rim_ref, w1_ref, w2_ref, l1, r1, oy1, iy1, l2, r2, oy2, iy2, edge_ref, cells_ref,
    lanes_ref, second_ref, pooled_ref, m1_ref, m2_ref, first_ref, sums_ref,
):
    chans, planes_in, size_y, depth = own_ref.shape
    size_x = second_ref.shape[0]
    group = 2
    build_matrix(w1_ref, l1, r1, oy1, iy1, m1_ref)
    build_matrix(w2_ref, l2, r2, oy2, iy2, m2_ref)
    rows1 = first_ref.shape[1]
    rows2 = second_ref.shape[1]

    def one(step, carry):
        at = step * group
        planes = []
        for k in range(group + 2):
            own = own_ref[:, at + k].reshape(chans * size_y, depth)
            planes.append(jnp.concatenate([own, rim_ref[at + k]], axis=0))
        data = stack_planes(planes, group)
        parts = jnp.dot(m1_ref[...], data, preferred_element_type=jnp.float32)
        sums = shift_sum(parts, rows1, group, depth)
        for k in range(group):
            first_ref[at + k] = jnp.maximum(sums[k], 0.0).astype(jnp.bfloat16)
        return carry

    lax.fori_loop(0, (size_x + 2) // group, one, 0)
    first_ref[0] = first_ref[0] * edge_ref[0:1, :].astype(jnp.bfloat16)
    first_ref[size_x + 1] = first_ref[size_x + 1] * edge_ref[1:2, :].astype(jnp.bfloat16)
    sums_ref[...] = jnp.zeros_like(sums_ref)

    def two(step, carry):
        at = step * group
        data = stack_planes([first_ref[at + k] for k in range(group + 2)], group)
        parts = jnp.dot(m2_ref[...], data, preferred_element_type=jnp.float32)
        sums = shift_sum(parts, rows2, group, depth)
        total = None
        for k in range(group):
            value = jnp.maximum(sums[k], 0.0).astype(jnp.bfloat16)
            second_ref[at + k] = value
            value = value.astype(jnp.float32)
            total = value if total is None else total + value
        block = at // POOL
        sums_ref[block] = sums_ref[block] + total
        return carry

    lax.fori_loop(0, size_x // group, two, 0)
    for block in range(size_x // POOL):
        by_row = jnp.dot(
            cells_ref[...], sums_ref[block],
            precision=lax.Precision.HIGHEST, preferred_element_type=jnp.float32,
        )
        pooled_ref[block] = jnp.dot(
            by_row, lanes_ref[...],
            precision=lax.Precision.HIGHEST, preferred_element_type=jnp.float32,
        ) / float(POOL**3)


def fine(own, rim, w_first, w_second, size_x):
    chans, _, size_y, depth = own.shape
    along_x, along_y = lax.axis_size("gx"), lax.axis_size("gy")
    at_x, at_y = lax.axis_index("gx"), lax.axis_index("gy")
    l1, r1, oy1, iy1 = spread_maps(chans, size_y, 1, 2)
    l2, r2, oy2, iy2 = spread_maps(chans, size_y, 0, 1)
    beyond = ((at_y == 0) & (oy1 < 0)) | ((at_y == along_y - 1) & (oy1 >= size_y))
    oy1 = jnp.where(beyond, FAR, oy1)

    def by_offset(weight):
        taps = weight.reshape(3, 3, 3, chans, chans)
        return jnp.transpose(taps, (1, 2, 3, 0, 4)).reshape(3, 3 * chans, 3 * chans)

    edge = jnp.stack([at_x > 0, at_x < along_x - 1]).astype(jnp.float32)
    edge = jnp.broadcast_to(edge[:, None], (2, depth))
    cells = jnp.asarray(np.repeat(np.eye(chans, dtype=np.float32), size_y, axis=1))
    lanes = jnp.asarray(np.repeat(np.eye(depth // POOL, dtype=np.float32), POOL, axis=0))
    rows1, rows2 = l1.shape[0] // 3, l2.shape[0] // 3
    cols1, cols2 = r1.shape[1], r2.shape[1]
    spec = pl.BlockSpec(memory_space=pltpu.VMEM)
    flops = 2 * depth * (3 * rows1 * cols1 * (size_x + 2) + 3 * rows2 * cols2 * size_x)
    return pl.pallas_call(
        fine_kernel,
        out_shape=(
            jax.ShapeDtypeStruct((size_x, rows2, depth), jnp.bfloat16),
            jax.ShapeDtypeStruct((size_x // POOL, chans, depth // POOL), jnp.float32),
        ),
        in_specs=[spec] * 15,
        out_specs=(spec, spec),
        scratch_shapes=[
            pltpu.VMEM((3 * rows1, cols1), jnp.bfloat16),
            pltpu.VMEM((3 * rows2, cols2), jnp.bfloat16),
            pltpu.VMEM((size_x + 2, rows1, depth), jnp.bfloat16),
            pltpu.VMEM((size_x // POOL, rows2, depth), jnp.float32),
        ],
        compiler_params=pltpu.CompilerParams(vmem_limit_bytes=VMEM_LIMIT),
        cost_estimate=pl.CostEstimate(flops=flops, bytes_accessed=8_000_000, transcendentals=0),
        name="fine",
    )(
        own, rim, by_offset(w_first), by_offset(w_second),
        l1, r1, oy1, iy1, l2, r2, oy2, iy2, edge, cells, lanes,
    )


def join_kernel(second_ref, up_ref, matrix_ref, out_ref):
    planes, rows, depth = second_ref.shape
    chans, _, size_y, _ = out_ref.shape
    up = up_ref[0]
    up = jnp.concatenate([up] * 2, axis=1)
    for at in range(0, planes, 2):
        data = jnp.concatenate([second_ref[at], second_ref[at + 1]], axis=1)
        skip = jnp.dot(matrix_ref[...], data, preferred_element_type=jnp.float32)
        value = (skip + up).astype(jnp.bfloat16)
        for k in range(2):
            cut = value[:, k * depth : (k + 1) * depth]
            out_ref[:, at + k] = cut.reshape(chans, size_y, depth)


def join(second, up, w_skip):
    size_x, rows, depth = second.shape
    chans = w_skip.shape[0]
    size_y = rows // chans
    up = jnp.repeat(jnp.repeat(up, POOL, axis=2), size_y, axis=1)
    matrix = w_skip[:, None, :, None] * jnp.eye(size_y, dtype=w_skip.dtype)[None, :, None, :]
    matrix = matrix.reshape(rows, rows)
    step = 8
    return pl.pallas_call(
        join_kernel,
        grid=(size_x // step,),
        out_shape=jax.ShapeDtypeStruct((chans, size_x, size_y, depth), jnp.bfloat16),
        in_specs=[
            pl.BlockSpec((step, rows, depth), lambda i: (i, 0, 0)),
            pl.BlockSpec((1, rows, depth), lambda i: (i * step // POOL, 0, 0)),
            pl.BlockSpec((rows, rows), lambda i: (0, 0)),
        ],
        out_specs=pl.BlockSpec((chans, step, size_y, depth), lambda i: (0, i, 0, 0)),
        compiler_params=pltpu.CompilerParams(vmem_limit_bytes=VMEM_LIMIT),
        cost_estimate=pl.CostEstimate(
            flops=2 * size_x * rows * rows * depth, bytes_accessed=5_000_000, transcendentals=0
        ),
        name="join",
    )(second, up, matrix)


def halo(features):
    chans, size_x, size_y, depth = features.shape
    nx, ny = lax.axis_size("gx"), lax.axis_size("gy")

    def both(axis, count, last, leading):
        up = [(i, i + 1) for i in range(count - 1)]
        down = [(j, i) for i, j in up]
        return lax.ppermute(last, axis, up), lax.ppermute(leading, axis, down)

    before, after = both("gx", nx, features[:, size_x - 2 :], features[:, :2])
    own = jnp.concatenate([before, features, after], axis=1)

    def side(v):
        return jnp.transpose(v, (1, 2, 0, 3)).reshape(size_x + 4, 2 * chans, depth)

    below, above = both("gy", ny, side(own[:, :, size_y - 2 :]), side(own[:, :, :2]))
    return own, jnp.concatenate([below, above], axis=1)


def coarse_level(pooled, w_lift, w_coarse, w_decode):
    block_x, chans, block_z = pooled.shape
    nx, ny = lax.axis_size("gx"), lax.axis_size("gy")
    at_x, at_y = lax.axis_index("gx"), lax.axis_index("gy")
    every = lax.all_gather(pooled, ("gx", "gy"), axis=0)
    every = every.reshape(nx, ny, block_x, chans, block_z)
    every = jnp.transpose(every, (0, 2, 1, 4, 3)).reshape(nx * block_x, ny, block_z, chans)
    every = jnp.pad(every, ((1, 1), (1, 1), (1, 1), (0, 0)))
    near = lax.dynamic_slice_in_dim(every, at_x * block_x, block_x + 2, axis=0)
    raised = jnp.einsum(
        "xyzc,oc->xyzo", near, w_lift.astype(jnp.float32), precision=lax.Precision.HIGHEST
    )
    lifted = jnp.maximum(raised, 0.0).astype(jnp.bfloat16)
    windows = []
    for offset in range(27):
        a, b, c = offset // 9, offset // 3 % 3, offset % 3
        cut = lifted[a : a + block_x, b : b + ny, c : c + block_z]
        windows.append(cut.reshape(block_x * ny * block_z, -1))
    stacked = jnp.concatenate(windows, axis=1)
    count = w_coarse.shape[0]
    total = lax.dot_general(
        stacked, w_coarse.reshape(count, -1), (((1,), (1,)), ((), ())),
        preferred_element_type=jnp.float32,
    )
    coarse = jnp.maximum(total, 0.0).astype(jnp.bfloat16)
    mine = lax.dynamic_slice_in_dim(w_decode, at_y * count, count, axis=1)
    part = lax.dot_general(
        coarse, mine, (((1,), (1,)), ((), ())), preferred_element_type=jnp.float32
    )
    part = jnp.transpose(part.reshape(block_x, ny, block_z, chans), (1, 0, 3, 2))
    whole = lax.psum_scatter(part, "gy", scatter_dimension=0, tiled=False)
    return whole.astype(jnp.bfloat16)


def local(features, w_first, w_second, w_lift, w_coarse, w_decode, w_joining):
    chans, size_x, size_y, depth = features.shape
    own, rim = halo(features)
    second, pooled = fine(own, rim, w_first, w_second, size_x)
    decoded = coarse_level(pooled, w_lift, w_coarse, w_decode)
    up = jnp.einsum(
        "oc,xcz->xoz", w_joining[:, chans:], decoded, preferred_element_type=jnp.float32
    )
    return join(second, up, w_joining[:, :chans])


def solution(mesh):
    in_specs = (P(None, "gx", "gy", None), P(), P(), P(), P("gy", None, None), P(), P())
    out_specs = P(None, "gx", "gy", None)
    return jax.shard_map(local, mesh=mesh, in_specs=in_specs, out_specs=out_specs, check_vma=False)
```

```python
import jax
import jax.numpy as jnp
import numpy as np
from jax import lax
from jax.experimental import pallas as pl
from jax.experimental.pallas import tpu as pltpu
from jax.sharding import PartitionSpec as P

POOL = 16
FAR = 4096
LANES = 128
MESH = pl.DeviceIdType.MESH
VMEM_LIMIT = 48 * 1024 * 1024


def rows_of(chans, size_y, width):
    own_c = np.repeat(np.arange(chans), size_y)
    own_y = np.tile(np.arange(size_y), chans)
    side_y = list(range(-width, 0)) + list(range(size_y, size_y + width))
    rim_c = np.tile(np.arange(chans), len(side_y))
    rim_y = np.repeat(np.array(side_y, dtype=np.int64), chans)
    return np.concatenate([own_c, rim_c]), np.concatenate([own_y, rim_y])


def spread_maps(chans, size_y, out_width, in_width):
    out_c, out_y = rows_of(chans, size_y, out_width)
    in_c, in_y = rows_of(chans, size_y, in_width)
    rows, cols = len(out_c), len(in_c)
    left = np.zeros((3 * rows, 3 * chans), np.float32)
    right = np.zeros((3 * chans, 3 * cols), np.float32)
    for tap in range(3):
        left[tap * rows + np.arange(rows), tap * chans + out_c] = 1.0
        right[tap * chans + in_c, tap * cols + np.arange(cols)] = 1.0
    as_bf = lambda v: jnp.asarray(v, jnp.bfloat16)
    return (
        as_bf(left),
        as_bf(right),
        jnp.asarray(np.tile(out_y, 3)[:, None], jnp.int32),
        jnp.asarray(np.tile(in_y, 3)[None, :], jnp.int32),
    )


def build_matrix(weight_ref, left_ref, right_ref, out_y_ref, in_y_ref, matrix_ref):
    gap = in_y_ref[...] - out_y_ref[...]
    total = jnp.zeros(matrix_ref.shape, jnp.float32)
    for shift_b in range(3):
        part = jnp.dot(left_ref[...], weight_ref[shift_b], preferred_element_type=jnp.float32)
        part = jnp.dot(
            part.astype(jnp.bfloat16), right_ref[...], preferred_element_type=jnp.float32
        )
        total = jnp.where(gap == shift_b - 1, part, total)
    matrix_ref[...] = total.astype(jnp.bfloat16)


def shift_sum(parts, rows, group, depth):
    lane = lax.broadcasted_iota(jnp.int32, (rows, depth), 1)
    planes = []
    for plane in range(group):
        cut = parts[:, plane * depth : (plane + 1) * depth]
        before = jnp.where(lane == 0, 0.0, pltpu.roll(cut[:rows], 1, 1))
        after = jnp.where(lane == depth - 1, 0.0, pltpu.roll(cut[2 * rows :], depth - 1, 1))
        planes.append(before + cut[rows : 2 * rows] + after)
    return planes


def stack_planes(planes, group):
    return jnp.concatenate(
        [jnp.concatenate(planes[a : a + group], axis=1) for a in range(3)], axis=0
    )


def nt_dot(a, b, precision=None, transposed=True):
    return lax.dot_general(
        a, b, (((1,), (1 if transposed else 0,)), ((), ())),
        precision=precision, preferred_element_type=jnp.float32,
    )


def fine_kernel(
    own_ref, rim_ref, w1_ref, w2_ref, l1, r1, oy1, iy1, l2, r2, oy2, iy2, edge_ref, cells_ref,
    lanes_ref, second_ref, pooled_ref, m1_ref, m2_ref, first_ref, sums_ref,
):
    chans, planes_in, size_y, depth = own_ref.shape
    size_x = second_ref.shape[0]
    group = 2
    build_matrix(w1_ref, l1, r1, oy1, iy1, m1_ref)
    build_matrix(w2_ref, l2, r2, oy2, iy2, m2_ref)
    rows1 = first_ref.shape[1]
    rows2 = second_ref.shape[1]

    def one(step, carry):
        at = step * group
        planes = []
        for k in range(group + 2):
            own = own_ref[:, at + k].reshape(chans * size_y, depth)
            planes.append(jnp.concatenate([own, rim_ref[at + k]], axis=0))
        data = stack_planes(planes, group)
        parts = jnp.dot(m1_ref[...], data, preferred_element_type=jnp.float32)
        sums = shift_sum(parts, rows1, group, depth)
        for k in range(group):
            first_ref[at + k] = jnp.maximum(sums[k], 0.0).astype(jnp.bfloat16)
        return carry

    lax.fori_loop(0, (size_x + 2) // group, one, 0)
    first_ref[0] = first_ref[0] * edge_ref[0:1, :].astype(jnp.bfloat16)
    first_ref[size_x + 1] = first_ref[size_x + 1] * edge_ref[1:2, :].astype(jnp.bfloat16)
    sums_ref[...] = jnp.zeros_like(sums_ref)

    def two(step, carry):
        at = step * group
        data = stack_planes([first_ref[at + k] for k in range(group + 2)], group)
        parts = jnp.dot(m2_ref[...], data, preferred_element_type=jnp.float32)
        sums = shift_sum(parts, rows2, group, depth)
        total = None
        for k in range(group):
            value = jnp.maximum(sums[k], 0.0).astype(jnp.bfloat16)
            second_ref[at + k] = value
            value = value.astype(jnp.float32)
            total = value if total is None else total + value
        block = at // POOL
        sums_ref[block] = sums_ref[block] + total
        return carry

    lax.fori_loop(0, size_x // group, two, 0)
    for block in range(size_x // POOL):
        by_row = jnp.dot(
            cells_ref[...], sums_ref[block],
            precision=lax.Precision.HIGHEST, preferred_element_type=jnp.float32,
        )
        pooled_ref[block] = nt_dot(
            lanes_ref[...], jnp.transpose(by_row), lax.Precision.HIGHEST, False
        ) / float(POOL**3)


def fine(own, rim, w_first, w_second, size_x):
    chans, _, size_y, depth = own.shape
    along_x, along_y = lax.axis_size("gx"), lax.axis_size("gy")
    at_x, at_y = lax.axis_index("gx"), lax.axis_index("gy")
    l1, r1, oy1, iy1 = spread_maps(chans, size_y, 1, 2)
    l2, r2, oy2, iy2 = spread_maps(chans, size_y, 0, 1)
    beyond = ((at_y == 0) & (oy1 < 0)) | ((at_y == along_y - 1) & (oy1 >= size_y))
    oy1 = jnp.where(beyond, FAR, oy1)

    def by_offset(weight):
        taps = weight.reshape(3, 3, 3, chans, chans)
        return jnp.transpose(taps, (1, 2, 3, 0, 4)).reshape(3, 3 * chans, 3 * chans)

    edge = jnp.stack([at_x > 0, at_x < along_x - 1]).astype(jnp.float32)
    edge = jnp.broadcast_to(edge[:, None], (2, depth))
    cells = np.repeat(np.eye(chans, dtype=np.float32), size_y, axis=1)
    cells = jnp.asarray(np.pad(cells, ((0, LANES - chans), (0, 0))))
    lanes = jnp.asarray(np.repeat(np.eye(depth // POOL, dtype=np.float32), POOL, axis=1))
    rows1, rows2 = l1.shape[0] // 3, l2.shape[0] // 3
    cols1, cols2 = r1.shape[1], r2.shape[1]
    spec = pl.BlockSpec(memory_space=pltpu.VMEM)
    flops = 2 * depth * (3 * rows1 * cols1 * (size_x + 2) + 3 * rows2 * cols2 * size_x)
    return pl.pallas_call(
        fine_kernel,
        out_shape=(
            jax.ShapeDtypeStruct((size_x, rows2, depth), jnp.bfloat16),
            jax.ShapeDtypeStruct((size_x // POOL, depth // POOL, LANES), jnp.float32),
        ),
        in_specs=[spec] * 15,
        out_specs=(spec, spec),
        scratch_shapes=[
            pltpu.VMEM((3 * rows1, cols1), jnp.bfloat16),
            pltpu.VMEM((3 * rows2, cols2), jnp.bfloat16),
            pltpu.VMEM((size_x + 2, rows1, depth), jnp.bfloat16),
            pltpu.VMEM((size_x // POOL, rows2, depth), jnp.float32),
        ],
        compiler_params=pltpu.CompilerParams(vmem_limit_bytes=VMEM_LIMIT),
        cost_estimate=pl.CostEstimate(flops=flops, bytes_accessed=8_000_000, transcendentals=0),
        name="fine",
    )(
        own, rim, by_offset(w_first), by_offset(w_second),
        l1, r1, oy1, iy1, l2, r2, oy2, iy2, edge, cells, lanes,
    )


def join_kernel(second_ref, up_ref, matrix_ref, out_ref):
    planes, rows, depth = second_ref.shape
    chans, _, size_y, _ = out_ref.shape
    up = up_ref[0]
    up = jnp.concatenate([up] * 2, axis=1)
    for at in range(0, planes, 2):
        data = jnp.concatenate([second_ref[at], second_ref[at + 1]], axis=1)
        skip = jnp.dot(matrix_ref[...], data, preferred_element_type=jnp.float32)
        value = (skip + up).astype(jnp.bfloat16)
        for k in range(2):
            cut = value[:, k * depth : (k + 1) * depth]
            out_ref[:, at + k] = cut.reshape(chans, size_y, depth)


def join(second, up, w_skip):
    size_x, rows, depth = second.shape
    chans = w_skip.shape[0]
    size_y = rows // chans
    matrix = w_skip[:, None, :, None] * jnp.eye(size_y, dtype=w_skip.dtype)[None, :, None, :]
    matrix = matrix.reshape(rows, rows)
    step = 8
    return pl.pallas_call(
        join_kernel,
        grid=(size_x // step,),
        out_shape=jax.ShapeDtypeStruct((chans, size_x, size_y, depth), jnp.bfloat16),
        in_specs=[
            pl.BlockSpec((step, rows, depth), lambda i: (i, 0, 0)),
            pl.BlockSpec((1, rows, depth), lambda i: (i * step // POOL, 0, 0)),
            pl.BlockSpec((rows, rows), lambda i: (0, 0)),
        ],
        out_specs=pl.BlockSpec((chans, step, size_y, depth), lambda i: (0, i, 0, 0)),
        compiler_params=pltpu.CompilerParams(vmem_limit_bytes=VMEM_LIMIT),
        cost_estimate=pl.CostEstimate(
            flops=2 * size_x * rows * rows * depth, bytes_accessed=5_000_000, transcendentals=0
        ),
        name="join",
    )(second, up, matrix)


def halo_kernel(nx, ny, features_ref, side_ref, zero_ref, zero_side_ref, own_ref, rim_ref, send, recv, local):
    at_x, at_y = lax.axis_index("gx"), lax.axis_index("gy")
    size_x = features_ref.shape[1]
    rows = side_ref.shape[2]

    def exists(dx, dy):
        x, y = at_x + dx, at_y + dy
        return (x >= 0) & (x < nx) & (y >= 0) & (y < ny)

    around = [(dx, dy) for dx in (-1, 0, 1) for dy in (-1, 0, 1) if (dx, dy) != (0, 0)]
    barrier = pltpu.get_barrier_semaphore()
    for dx, dy in around:

        @pl.when(exists(dx, dy))
        def _():
            pl.semaphore_signal(
                barrier, inc=1, device_id=(at_x + dx, at_y + dy), device_id_type=MESH
            )

    wide = 3 - (at_x == 0).astype(jnp.int32) - (at_x == nx - 1).astype(jnp.int32)
    high = 3 - (at_y == 0).astype(jnp.int32) - (at_y == ny - 1).astype(jnp.int32)
    pl.semaphore_wait(barrier, wide * high - 1)

    taken = {-1: (0, 2), 0: (0, size_x), 1: (size_x - 2, 2)}
    landed = {-1: (size_x + 2, 2), 0: (2, size_x), 1: (0, 2)}

    def place(dx, dy):
        start, count = landed[dx]
        if dy == 0:
            return own_ref.at[:, start : start + count]
        row = 0 if dy == 1 else rows
        return rim_ref.at[start : start + count, row : row + rows]

    def sent(index, dx, dy):
        start, count = taken[dx]
        if dy == 0:
            source = features_ref.at[:, start : start + count]
        else:
            source = side_ref.at[0 if dy == 1 else 1, start : start + count]
        return pltpu.make_async_remote_copy(
            src_ref=source, dst_ref=place(dx, dy), send_sem=send.at[index],
            recv_sem=recv.at[index],
            device_id=(lax.rem(at_x + dx + nx, nx), lax.rem(at_y + dy + ny, ny)),
            device_id_type=MESH,
        )

    def blank(index, dx, dy):
        count = landed[dx][1]
        source = zero_ref if dy == 0 else zero_side_ref.at[0:count]
        return pltpu.make_async_copy(source, place(dx, dy), local.at[index])

    for index, (dx, dy) in enumerate(around):

        @pl.when(exists(dx, dy))
        def _():
            sent(index, dx, dy).start()

        @pl.when(jnp.logical_not(exists(-dx, -dy)))
        def _():
            blank(index, dx, dy).start()

    middle = pltpu.make_async_copy(
        features_ref, own_ref.at[:, 2 : size_x + 2], local.at[len(around)]
    )
    middle.start()
    for index, (dx, dy) in enumerate(around):

        @pl.when(exists(-dx, -dy))
        def _():
            sent(index, dx, dy).wait_recv()

        @pl.when(jnp.logical_not(exists(-dx, -dy)))
        def _():
            blank(index, dx, dy).wait()

        @pl.when(exists(dx, dy))
        def _():
            sent(index, dx, dy).wait_send()

    middle.wait()


def halo(features):
    chans, size_x, size_y, depth = features.shape
    nx, ny = lax.axis_size("gx"), lax.axis_size("gy")

    def side(v):
        return jnp.transpose(v, (1, 2, 0, 3)).reshape(size_x, 2 * chans, depth)

    sides = jnp.stack([side(features[:, :, size_y - 2 :]), side(features[:, :, :2])])
    anywhere = pl.BlockSpec(memory_space=pl.ANY)
    return pl.pallas_call(
        lambda *refs: halo_kernel(nx, ny, *refs),
        out_shape=(
            jax.ShapeDtypeStruct((chans, size_x + 4, size_y, depth), jnp.bfloat16),
            jax.ShapeDtypeStruct((size_x + 4, 4 * chans, depth), jnp.bfloat16),
        ),
        in_specs=[anywhere] * 4,
        out_specs=(anywhere, anywhere),
        scratch_shapes=[
            pltpu.SemaphoreType.DMA((8,)),
            pltpu.SemaphoreType.DMA((8,)),
            pltpu.SemaphoreType.DMA((9,)),
        ],
        compiler_params=pltpu.CompilerParams(collective_id=0, has_side_effects=True),
        name="halo",
    )(
        features, sides, jnp.zeros((chans, 2, size_y, depth), jnp.bfloat16),
        jnp.zeros((size_x, 2 * chans, depth), jnp.bfloat16),
    )


def coarse_kernel(
    nx, ny, pooled_ref, lift_ref, weight_ref, decode_ref, join_ref, cells_ref, lanes_ref, up_ref,
    near_ref, field_ref, lifted_ref, part_ref, parts_ref,
    send_x, recv_x, send_y, recv_y, send_p, recv_p,
):
    at_x, at_y = lax.axis_index("gx"), lax.axis_index("gy")
    block_x, block_z, lanes = pooled_ref.shape
    peers = [lax.rem(at_y + step, ny) for step in range(1, ny)]
    has_low, has_high = at_x > 0, at_x < nx - 1

    barrier = pltpu.get_barrier_semaphore()
    for peer in peers:
        pl.semaphore_signal(barrier, inc=1, device_id=(at_x, peer), device_id_type=MESH)

    @pl.when(has_low)
    def _():
        pl.semaphore_signal(barrier, inc=1, device_id=(at_x - 1, at_y), device_id_type=MESH)

    @pl.when(has_high)
    def _():
        pl.semaphore_signal(barrier, inc=1, device_id=(at_x + 1, at_y), device_id_type=MESH)

    pl.semaphore_wait(
        barrier, ny - 1 + has_low.astype(jnp.int32) + has_high.astype(jnp.int32)
    )

    def beside(index):
        source, place, target = (
            (block_x - 1, 0, lax.rem(at_x + 1, nx)),
            (0, block_x + 1, lax.rem(at_x + nx - 1, nx)),
        )[index]
        return pltpu.make_async_remote_copy(
            src_ref=pooled_ref.at[source], dst_ref=near_ref.at[place],
            send_sem=send_x.at[index], recv_sem=recv_x.at[index],
            device_id=(target, at_y), device_id_type=MESH,
        )

    blank = jnp.zeros((block_z, lanes), jnp.float32)

    @pl.when(has_high)
    def _():
        beside(0).start()

    @pl.when(has_low)
    def _():
        beside(1).start()

    near_ref[1 : block_x + 1] = pooled_ref[...]
    field_ref[0] = jnp.zeros(field_ref.shape[1:], jnp.float32)
    field_ref[ny + 1] = jnp.zeros(field_ref.shape[1:], jnp.float32)
    lifted_ref[...] = jnp.zeros_like(lifted_ref)

    @pl.when(has_low)
    def _():
        beside(0).wait_recv()

    @pl.when(has_high)
    def _():
        beside(1).wait_recv()

    @pl.when(jnp.logical_not(has_low))
    def _():
        near_ref[0] = blank

    @pl.when(jnp.logical_not(has_high))
    def _():
        near_ref[block_x + 1] = blank

    gather = []
    for step, peer in enumerate(peers):
        copy = pltpu.make_async_remote_copy(
            src_ref=near_ref, dst_ref=field_ref.at[at_y + 1],
            send_sem=send_y.at[step], recv_sem=recv_y.at[step],
            device_id=(at_x, peer), device_id_type=MESH,
        )
        copy.start()
        gather.append(copy)
    field_ref[at_y + 1] = near_ref[...]
    for copy in gather:
        copy.wait_recv()

    field = field_ref[...].reshape((ny + 2) * (block_x + 2) * block_z, lanes)
    raised = nt_dot(field, lift_ref[...], lax.Precision.HIGHEST, False)
    raised = jnp.maximum(raised, 0.0).astype(jnp.bfloat16).astype(jnp.float32)
    wide = raised.shape[1]
    lifted_ref[:, :, block_z : 2 * block_z] = raised.reshape(ny + 2, block_x + 2, block_z, wide)
    count = ny * block_x * block_z
    total = jnp.zeros((count, weight_ref.shape[1]), jnp.float32)
    for offset in range(27):
        a, b, c = offset // 9, offset // 3 % 3, offset % 3
        low = block_z - 1 + c
        cut = lifted_ref[b : b + ny, a : a + block_x, low : low + block_z]
        cut = cut.reshape(count, wide).astype(jnp.bfloat16)
        total = total + nt_dot(cut, weight_ref[offset])
    coarse = jnp.maximum(total, 0.0).astype(jnp.bfloat16)
    part = jnp.dot(coarse, decode_ref[...], preferred_element_type=jnp.float32)
    part_ref[...] = part.reshape(part_ref.shape)
    scatter = []
    for step, peer in enumerate(peers):
        copy = pltpu.make_async_remote_copy(
            src_ref=part_ref.at[peer], dst_ref=parts_ref.at[at_y],
            send_sem=send_p.at[step], recv_sem=recv_p.at[step],
            device_id=(at_x, peer), device_id_type=MESH,
        )
        copy.start()
        scatter.append(copy)
    parts_ref[at_y] = part_ref[at_y]
    for copy in scatter:
        copy.wait_recv()
    decoded = jnp.sum(parts_ref[...], axis=0).astype(jnp.bfloat16)
    up = jnp.dot(decoded, join_ref[...], preferred_element_type=jnp.float32)
    for block in range(block_x):
        mine = up[block * block_z : (block + 1) * block_z]
        mine = nt_dot(jnp.transpose(mine), lanes_ref[...], lax.Precision.HIGHEST, False)
        up_ref[block] = nt_dot(cells_ref[...], mine, lax.Precision.HIGHEST, False)

    @pl.when(has_high)
    def _():
        beside(0).wait_send()

    @pl.when(has_low)
    def _():
        beside(1).wait_send()

    for copy in gather + scatter:
        copy.wait_send()


def coarse_level(pooled, w_lift, w_coarse, w_decode, w_up, size_y):
    block_x, block_z, lanes = pooled.shape
    nx, ny = lax.axis_size("gx"), lax.axis_size("gy")
    count, _, wide = w_coarse.shape
    chans = w_up.shape[0]
    more = lanes - chans
    lift = jnp.pad(w_lift.astype(jnp.float32).T, ((0, more), (0, 0)))
    mine = lax.dynamic_slice_in_dim(w_decode, lax.axis_index("gy") * count, count, axis=1)
    decode = jnp.pad(mine.T, ((0, 0), (0, more)))
    joining = jnp.pad(w_up.T, ((0, more), (0, more)))
    cells = np.repeat(np.eye(chans, dtype=np.float32), size_y, axis=0)
    cells = jnp.asarray(np.pad(cells, ((0, 0), (0, more))))
    spread = jnp.asarray(np.repeat(np.eye(block_z, dtype=np.float32), POOL, axis=1))
    spec = pl.BlockSpec(memory_space=pltpu.VMEM)
    vector = lambda *shape: pltpu.VMEM(shape, jnp.float32)
    return pl.pallas_call(
        lambda *refs: coarse_kernel(nx, ny, *refs),
        out_shape=jax.ShapeDtypeStruct((block_x, chans * size_y, block_z * POOL), jnp.float32),
        in_specs=[spec] * 7,
        out_specs=spec,
        scratch_shapes=[
            vector(block_x + 2, block_z, lanes),
            vector(ny + 2, block_x + 2, block_z, lanes),
            vector(ny + 2, block_x + 2, 3 * block_z, wide),
            vector(ny, block_x * block_z, lanes),
            vector(ny, block_x * block_z, lanes),
            pltpu.SemaphoreType.DMA((2,)),
            pltpu.SemaphoreType.DMA((2,)),
        ] + [pltpu.SemaphoreType.DMA((ny - 1,))] * 4,
        compiler_params=pltpu.CompilerParams(
            collective_id=1, has_side_effects=True, vmem_limit_bytes=VMEM_LIMIT
        ),
        name="coarse",
    )(
        pooled, lift, jnp.transpose(w_coarse, (1, 0, 2)), decode, joining, cells, spread,
    )


def local(features, w_first, w_second, w_lift, w_coarse, w_decode, w_joining):
    chans, size_x, size_y, depth = features.shape
    own, rim = halo(features)
    second, pooled = fine(own, rim, w_first, w_second, size_x)
    up = coarse_level(pooled, w_lift, w_coarse, w_decode, w_joining[:, chans:], size_y)
    return join(second, up, w_joining[:, :chans])


def solution(mesh):
    in_specs = (P(None, "gx", "gy", None), P(), P(), P(), P("gy", None, None), P(), P())
    out_specs = P(None, "gx", "gy", None)
    return jax.shard_map(local, mesh=mesh, in_specs=in_specs, out_specs=out_specs, check_vma=False)
```

```python
import jax
import jax.numpy as jnp
import numpy as np
from jax import lax
from jax.experimental import pallas as pl
from jax.experimental.pallas import tpu as pltpu
from jax.sharding import PartitionSpec as P

POOL = 16
FAR = 4096
LANES = 128
MESH = pl.DeviceIdType.MESH
VMEM_LIMIT = 48 * 1024 * 1024


def rows_of(chans, size_y, width):
    own_c = np.repeat(np.arange(chans), size_y)
    own_y = np.tile(np.arange(size_y), chans)
    side_y = list(range(-width, 0)) + list(range(size_y, size_y + width))
    rim_c = np.tile(np.arange(chans), len(side_y))
    rim_y = np.repeat(np.array(side_y, dtype=np.int64), chans)
    return np.concatenate([own_c, rim_c]), np.concatenate([own_y, rim_y])


def spread_maps(chans, size_y, out_width, in_width):
    out_c, out_y = rows_of(chans, size_y, out_width)
    in_c, in_y = rows_of(chans, size_y, in_width)
    rows, cols = len(out_c), len(in_c)
    left = np.zeros((3 * rows, 3 * chans), np.float32)
    right = np.zeros((3 * chans, 3 * cols), np.float32)
    for tap in range(3):
        left[tap * rows + np.arange(rows), tap * chans + out_c] = 1.0
        right[tap * chans + in_c, tap * cols + np.arange(cols)] = 1.0
    as_bf = lambda v: jnp.asarray(v, jnp.bfloat16)
    return (
        as_bf(left),
        as_bf(right),
        jnp.asarray(np.tile(out_y, 3)[:, None], jnp.int32),
        jnp.asarray(np.tile(in_y, 3)[None, :], jnp.int32),
    )


def build_matrix(weight_ref, left_ref, right_ref, out_y_ref, in_y_ref, matrix_ref):
    gap = in_y_ref[...] - out_y_ref[...]
    total = jnp.zeros(matrix_ref.shape, jnp.float32)
    for shift_b in range(3):
        part = jnp.dot(left_ref[...], weight_ref[shift_b], preferred_element_type=jnp.float32)
        part = jnp.dot(
            part.astype(jnp.bfloat16), right_ref[...], preferred_element_type=jnp.float32
        )
        total = jnp.where(gap == shift_b - 1, part, total)
    matrix_ref[...] = total.astype(jnp.bfloat16)


def shift_sum(parts, rows, group, depth):
    lane = lax.broadcasted_iota(jnp.int32, (rows, depth), 1)
    planes = []
    for plane in range(group):
        cut = parts[:, plane * depth : (plane + 1) * depth]
        before = jnp.where(lane == 0, 0.0, pltpu.roll(cut[:rows], 1, 1))
        after = jnp.where(lane == depth - 1, 0.0, pltpu.roll(cut[2 * rows :], depth - 1, 1))
        planes.append(before + cut[rows : 2 * rows] + after)
    return planes


def stack_planes(planes, group):
    return jnp.concatenate(
        [jnp.concatenate(planes[a : a + group], axis=1) for a in range(3)], axis=0
    )


def nt_dot(a, b, precision=None, transposed=True):
    return lax.dot_general(
        a, b, (((1,), (1 if transposed else 0,)), ((), ())),
        precision=precision, preferred_element_type=jnp.float32,
    )


def in_pairs(body, steps, group):
    def pair(step, carry):
        body(step * 2 * group)
        body(step * 2 * group + group)
        return carry

    lax.fori_loop(0, steps // 2, pair, 0)
    if steps % 2:
        body((steps - 1) * group)


def fine_kernel(
    features_ref, beyond_ref, rim_ref, w1_ref, w2_ref, l1, r1, oy1, iy1, l2, r2, oy2, iy2, edge_ref, cells_ref,
    lanes_ref, second_ref, pooled_ref, m1_ref, m2_ref, first_ref, sums_ref,
    own_ref,
):
    chans, size_x, size_y, depth = features_ref.shape
    own_ref[:, 0:2] = beyond_ref[0]
    own_ref[:, 2 : size_x + 2] = features_ref[...]
    own_ref[:, size_x + 2 :] = beyond_ref[1]
    group = 2
    build_matrix(w1_ref, l1, r1, oy1, iy1, m1_ref)
    build_matrix(w2_ref, l2, r2, oy2, iy2, m2_ref)
    rows1 = first_ref.shape[1]
    rows2 = second_ref.shape[1]

    def one(at):
        planes = []
        for k in range(group + 2):
            own = own_ref[:, at + k].reshape(chans * size_y, depth)
            planes.append(jnp.concatenate([own, rim_ref[at + k]], axis=0))
        data = stack_planes(planes, group)
        parts = jnp.dot(m1_ref[...], data, preferred_element_type=jnp.float32)
        sums = shift_sum(parts, rows1, group, depth)
        for k in range(group):
            first_ref[at + k] = jnp.maximum(sums[k], 0.0).astype(jnp.bfloat16)

    in_pairs(one, (size_x + 2) // group, group)
    first_ref[0] = first_ref[0] * edge_ref[0:1, :].astype(jnp.bfloat16)
    first_ref[size_x + 1] = first_ref[size_x + 1] * edge_ref[1:2, :].astype(jnp.bfloat16)
    sums_ref[...] = jnp.zeros_like(sums_ref)

    def two(at):
        data = stack_planes([first_ref[at + k] for k in range(group + 2)], group)
        parts = jnp.dot(m2_ref[...], data, preferred_element_type=jnp.float32)
        sums = shift_sum(parts, rows2, group, depth)
        total = None
        for k in range(group):
            value = jnp.maximum(sums[k], 0.0).astype(jnp.bfloat16)
            second_ref[at + k] = value
            value = value.astype(jnp.float32)
            total = value if total is None else total + value
        block = at // POOL
        sums_ref[block] = sums_ref[block] + total

    in_pairs(two, size_x // group, group)
    for block in range(size_x // POOL):
        by_row = jnp.dot(
            cells_ref[...], sums_ref[block],
            precision=lax.Precision.HIGHEST, preferred_element_type=jnp.float32,
        )
        pooled_ref[block] = nt_dot(
            lanes_ref[...], jnp.transpose(by_row), lax.Precision.HIGHEST, False
        ) / float(POOL**3)


def fine(features, beyond, rim, w_first, w_second):
    chans, size_x, size_y, depth = features.shape
    along_x, along_y = lax.axis_size("gx"), lax.axis_size("gy")
    at_x, at_y = lax.axis_index("gx"), lax.axis_index("gy")
    l1, r1, oy1, iy1 = spread_maps(chans, size_y, 1, 2)
    l2, r2, oy2, iy2 = spread_maps(chans, size_y, 0, 1)
    outside = ((at_y == 0) & (oy1 < 0)) | ((at_y == along_y - 1) & (oy1 >= size_y))
    oy1 = jnp.where(outside, FAR, oy1)

    def by_offset(weight):
        taps = weight.reshape(3, 3, 3, chans, chans)
        return jnp.transpose(taps, (1, 2, 3, 0, 4)).reshape(3, 3 * chans, 3 * chans)

    edge = jnp.stack([at_x > 0, at_x < along_x - 1]).astype(jnp.float32)
    edge = jnp.broadcast_to(edge[:, None], (2, depth))
    cells = np.repeat(np.eye(chans, dtype=np.float32), size_y, axis=1)
    cells = jnp.asarray(np.pad(cells, ((0, LANES - chans), (0, 0))))
    lanes = jnp.asarray(np.repeat(np.eye(depth // POOL, dtype=np.float32), POOL, axis=1))
    rows1, rows2 = l1.shape[0] // 3, l2.shape[0] // 3
    cols1, cols2 = r1.shape[1], r2.shape[1]
    spec = pl.BlockSpec(memory_space=pltpu.VMEM)
    flops = 2 * depth * (3 * rows1 * cols1 * (size_x + 2) + 3 * rows2 * cols2 * size_x)
    return pl.pallas_call(
        fine_kernel,
        out_shape=(
            jax.ShapeDtypeStruct((size_x, rows2, depth), jnp.bfloat16),
            jax.ShapeDtypeStruct((size_x // POOL, depth // POOL, LANES), jnp.float32),
        ),
        in_specs=[spec] * 16,
        out_specs=(spec, spec),
        scratch_shapes=[
            pltpu.VMEM((3 * rows1, cols1), jnp.bfloat16),
            pltpu.VMEM((3 * rows2, cols2), jnp.bfloat16),
            pltpu.VMEM((size_x + 2, rows1, depth), jnp.bfloat16),
            pltpu.VMEM((size_x // POOL, rows2, depth), jnp.float32),
            pltpu.VMEM((chans, size_x + 4, size_y, depth), jnp.bfloat16),
        ],
        compiler_params=pltpu.CompilerParams(vmem_limit_bytes=VMEM_LIMIT),
        cost_estimate=pl.CostEstimate(flops=flops, bytes_accessed=8_000_000, transcendentals=0),
        name="fine",
    )(
        features, beyond, rim, by_offset(w_first), by_offset(w_second),
        l1, r1, oy1, iy1, l2, r2, oy2, iy2, edge, cells, lanes,
    )


def join_kernel(second_ref, up_ref, matrix_ref, out_ref):
    planes, rows, depth = second_ref.shape
    chans, _, size_y, _ = out_ref.shape
    up = up_ref[0]
    up = jnp.concatenate([up] * 2, axis=1)
    for at in range(0, planes, 2):
        data = jnp.concatenate([second_ref[at], second_ref[at + 1]], axis=1)
        skip = jnp.dot(matrix_ref[...], data, preferred_element_type=jnp.float32)
        value = (skip + up).astype(jnp.bfloat16)
        for k in range(2):
            cut = value[:, k * depth : (k + 1) * depth]
            out_ref[:, at + k] = cut.reshape(chans, size_y, depth)


def join(second, up, w_skip):
    size_x, rows, depth = second.shape
    chans = w_skip.shape[0]
    size_y = rows // chans
    matrix = w_skip[:, None, :, None] * jnp.eye(size_y, dtype=w_skip.dtype)[None, :, None, :]
    matrix = matrix.reshape(rows, rows)
    step = 8
    return pl.pallas_call(
        join_kernel,
        grid=(size_x // step,),
        out_shape=jax.ShapeDtypeStruct((chans, size_x, size_y, depth), jnp.bfloat16),
        in_specs=[
            pl.BlockSpec((step, rows, depth), lambda i: (i, 0, 0)),
            pl.BlockSpec((1, rows, depth), lambda i: (i * step // POOL, 0, 0)),
            pl.BlockSpec((rows, rows), lambda i: (0, 0)),
        ],
        out_specs=pl.BlockSpec((chans, step, size_y, depth), lambda i: (0, i, 0, 0)),
        compiler_params=pltpu.CompilerParams(vmem_limit_bytes=VMEM_LIMIT),
        cost_estimate=pl.CostEstimate(
            flops=2 * size_x * rows * rows * depth, bytes_accessed=5_000_000, transcendentals=0
        ),
        name="join",
    )(second, up, matrix)


def halo_kernel(nx, ny, features_ref, side_ref, beyond_out, rim_out, beyond_ref, rim_ref, send, recv):
    at_x, at_y = lax.axis_index("gx"), lax.axis_index("gy")
    size_x = features_ref.shape[1]
    rows = side_ref.shape[2]

    def exists(dx, dy):
        x, y = at_x + dx, at_y + dy
        return (x >= 0) & (x < nx) & (y >= 0) & (y < ny)

    around = [(dx, dy) for dx in (-1, 0, 1) for dy in (-1, 0, 1) if (dx, dy) != (0, 0)]
    barrier = pltpu.get_barrier_semaphore()
    for dx, dy in around:

        @pl.when(exists(dx, dy))
        def _():
            pl.semaphore_signal(
                barrier, inc=1, device_id=(at_x + dx, at_y + dy), device_id_type=MESH
            )

    wide = 3 - (at_x == 0).astype(jnp.int32) - (at_x == nx - 1).astype(jnp.int32)
    high = 3 - (at_y == 0).astype(jnp.int32) - (at_y == ny - 1).astype(jnp.int32)
    pl.semaphore_wait(barrier, wide * high - 1)

    taken = {-1: (0, 2), 0: (0, size_x), 1: (size_x - 2, 2)}
    landed = {-1: (size_x + 2, 2), 0: (2, size_x), 1: (0, 2)}

    def place(dx, dy):
        start, count = landed[dx]
        if dy == 0:
            return beyond_ref.at[0 if dx == 1 else 1]
        row = 0 if dy == 1 else rows
        return rim_ref.at[start : start + count, row : row + rows]

    def sent(index, dx, dy):
        start, count = taken[dx]
        if dy == 0:
            source = features_ref.at[:, start : start + count]
        else:
            source = side_ref.at[0 if dy == 1 else 1, start : start + count]
        return pltpu.make_async_remote_copy(
            src_ref=source, dst_ref=place(dx, dy), send_sem=send.at[index],
            recv_sem=recv.at[index],
            device_id=(lax.rem(at_x + dx + nx, nx), lax.rem(at_y + dy + ny, ny)),
            device_id_type=MESH,
        )

    for index, (dx, dy) in enumerate(around):

        @pl.when(exists(dx, dy))
        def _():
            sent(index, dx, dy).start()

        @pl.when(jnp.logical_not(exists(-dx, -dy)))
        def _():
            spot = place(dx, dy)
            spot[...] = jnp.zeros(spot.shape, spot.dtype)

    for index, (dx, dy) in enumerate(around):

        @pl.when(exists(-dx, -dy))
        def _():
            sent(index, dx, dy).wait_recv()

        @pl.when(exists(dx, dy))
        def _():
            sent(index, dx, dy).wait_send()

    beyond_out[...] = beyond_ref[...]
    rim_out[...] = rim_ref[...]


def halo(features):
    chans, size_x, size_y, depth = features.shape
    nx, ny = lax.axis_size("gx"), lax.axis_size("gy")

    def side(v):
        return jnp.transpose(v, (1, 2, 0, 3)).reshape(size_x, 2 * chans, depth)

    sides = jnp.stack([side(features[:, :, size_y - 2 :]), side(features[:, :, :2])])
    anywhere = pl.BlockSpec(memory_space=pl.ANY)
    within = pl.BlockSpec(memory_space=pltpu.VMEM)
    return pl.pallas_call(
        lambda *refs: halo_kernel(nx, ny, *refs),
        out_shape=(
            jax.ShapeDtypeStruct((2, chans, 2, size_y, depth), jnp.bfloat16),
            jax.ShapeDtypeStruct((size_x + 4, 4 * chans, depth), jnp.bfloat16),
        ),
        in_specs=[anywhere] * 2,
        out_specs=(within, within),
        scratch_shapes=[
            pltpu.VMEM((2, chans, 2, size_y, depth), jnp.bfloat16),
            pltpu.VMEM((size_x + 4, 4 * chans, depth), jnp.bfloat16),
            pltpu.SemaphoreType.DMA((8,)),
            pltpu.SemaphoreType.DMA((8,)),
        ],
        compiler_params=pltpu.CompilerParams(collective_id=0, has_side_effects=True),
        name="halo",
    )(features, sides)


def coarse_kernel(
    nx, ny, pooled_ref, lift_ref, weight_ref, decode_ref, join_ref, cells_ref, lanes_ref, up_ref,
    near_ref, field_ref, lifted_ref, part_ref, parts_ref,
    send_x, recv_x, send_y, recv_y, send_p, recv_p,
):
    at_x, at_y = lax.axis_index("gx"), lax.axis_index("gy")
    block_x, block_z, lanes = pooled_ref.shape
    peers = [lax.rem(at_y + step, ny) for step in range(1, ny)]
    has_low, has_high = at_x > 0, at_x < nx - 1

    barrier = pltpu.get_barrier_semaphore()
    for peer in peers:
        pl.semaphore_signal(barrier, inc=1, device_id=(at_x, peer), device_id_type=MESH)

    @pl.when(has_low)
    def _():
        pl.semaphore_signal(barrier, inc=1, device_id=(at_x - 1, at_y), device_id_type=MESH)

    @pl.when(has_high)
    def _():
        pl.semaphore_signal(barrier, inc=1, device_id=(at_x + 1, at_y), device_id_type=MESH)

    pl.semaphore_wait(
        barrier, ny - 1 + has_low.astype(jnp.int32) + has_high.astype(jnp.int32)
    )

    def beside(index):
        source, place, target = (
            (block_x - 1, 0, lax.rem(at_x + 1, nx)),
            (0, block_x + 1, lax.rem(at_x + nx - 1, nx)),
        )[index]
        return pltpu.make_async_remote_copy(
            src_ref=pooled_ref.at[source], dst_ref=near_ref.at[place],
            send_sem=send_x.at[index], recv_sem=recv_x.at[index],
            device_id=(target, at_y), device_id_type=MESH,
        )

    blank = jnp.zeros((block_z, lanes), jnp.float32)

    @pl.when(has_high)
    def _():
        beside(0).start()

    @pl.when(has_low)
    def _():
        beside(1).start()

    near_ref[1 : block_x + 1] = pooled_ref[...]
    field_ref[0] = jnp.zeros(field_ref.shape[1:], jnp.float32)
    field_ref[ny + 1] = jnp.zeros(field_ref.shape[1:], jnp.float32)
    lifted_ref[...] = jnp.zeros_like(lifted_ref)

    @pl.when(has_low)
    def _():
        beside(0).wait_recv()

    @pl.when(has_high)
    def _():
        beside(1).wait_recv()

    @pl.when(jnp.logical_not(has_low))
    def _():
        near_ref[0] = blank

    @pl.when(jnp.logical_not(has_high))
    def _():
        near_ref[block_x + 1] = blank

    gather = []
    for step, peer in enumerate(peers):
        copy = pltpu.make_async_remote_copy(
            src_ref=near_ref, dst_ref=field_ref.at[at_y + 1],
            send_sem=send_y.at[step], recv_sem=recv_y.at[step],
            device_id=(at_x, peer), device_id_type=MESH,
        )
        copy.start()
        gather.append(copy)
    field_ref[at_y + 1] = near_ref[...]
    for copy in gather:
        copy.wait_recv()

    field = field_ref[...].reshape((ny + 2) * (block_x + 2) * block_z, lanes)
    raised = nt_dot(field, lift_ref[...], lax.Precision.HIGHEST, False)
    raised = jnp.maximum(raised, 0.0).astype(jnp.bfloat16).astype(jnp.float32)
    wide = raised.shape[1]
    lifted_ref[:, :, block_z : 2 * block_z] = raised.reshape(ny + 2, block_x + 2, block_z, wide)
    count = ny * block_x * block_z
    total = jnp.zeros((count, weight_ref.shape[1]), jnp.float32)
    for offset in range(27):
        a, b, c = offset // 9, offset // 3 % 3, offset % 3
        low = block_z - 1 + c
        cut = lifted_ref[b : b + ny, a : a + block_x, low : low + block_z]
        cut = cut.reshape(count, wide).astype(jnp.bfloat16)
        total = total + nt_dot(cut, weight_ref[offset])
    coarse = jnp.maximum(total, 0.0).astype(jnp.bfloat16)
    part = jnp.dot(coarse, decode_ref[...], preferred_element_type=jnp.float32)
    part_ref[...] = part.reshape(part_ref.shape)
    scatter = []
    for step, peer in enumerate(peers):
        copy = pltpu.make_async_remote_copy(
            src_ref=part_ref.at[peer], dst_ref=parts_ref.at[at_y],
            send_sem=send_p.at[step], recv_sem=recv_p.at[step],
            device_id=(at_x, peer), device_id_type=MESH,
        )
        copy.start()
        scatter.append(copy)
    parts_ref[at_y] = part_ref[at_y]
    for copy in scatter:
        copy.wait_recv()
    decoded = jnp.sum(parts_ref[...], axis=0).astype(jnp.bfloat16)
    up = jnp.dot(decoded, join_ref[...], preferred_element_type=jnp.float32)
    for block in range(block_x):
        mine = up[block * block_z : (block + 1) * block_z]
        mine = nt_dot(jnp.transpose(mine), lanes_ref[...], lax.Precision.HIGHEST, False)
        up_ref[block] = nt_dot(cells_ref[...], mine, lax.Precision.HIGHEST, False)

    @pl.when(has_high)
    def _():
        beside(0).wait_send()

    @pl.when(has_low)
    def _():
        beside(1).wait_send()

    for copy in gather + scatter:
        copy.wait_send()


def coarse_level(pooled, w_lift, w_coarse, w_decode, w_up, size_y):
    block_x, block_z, lanes = pooled.shape
    nx, ny = lax.axis_size("gx"), lax.axis_size("gy")
    count, _, wide = w_coarse.shape
    chans = w_up.shape[0]
    more = lanes - chans
    lift = jnp.pad(w_lift.astype(jnp.float32).T, ((0, more), (0, 0)))
    mine = lax.dynamic_slice_in_dim(w_decode, lax.axis_index("gy") * count, count, axis=1)
    decode = jnp.pad(mine.T, ((0, 0), (0, more)))
    joining = jnp.pad(w_up.T, ((0, more), (0, more)))
    cells = np.repeat(np.eye(chans, dtype=np.float32), size_y, axis=0)
    cells = jnp.asarray(np.pad(cells, ((0, 0), (0, more))))
    spread = jnp.asarray(np.repeat(np.eye(block_z, dtype=np.float32), POOL, axis=1))
    spec = pl.BlockSpec(memory_space=pltpu.VMEM)
    vector = lambda *shape: pltpu.VMEM(shape, jnp.float32)
    return pl.pallas_call(
        lambda *refs: coarse_kernel(nx, ny, *refs),
        out_shape=jax.ShapeDtypeStruct((block_x, chans * size_y, block_z * POOL), jnp.float32),
        in_specs=[spec] * 7,
        out_specs=spec,
        scratch_shapes=[
            vector(block_x + 2, block_z, lanes),
            vector(ny + 2, block_x + 2, block_z, lanes),
            vector(ny + 2, block_x + 2, 3 * block_z, wide),
            vector(ny, block_x * block_z, lanes),
            vector(ny, block_x * block_z, lanes),
            pltpu.SemaphoreType.DMA((2,)),
            pltpu.SemaphoreType.DMA((2,)),
        ] + [pltpu.SemaphoreType.DMA((ny - 1,))] * 4,
        compiler_params=pltpu.CompilerParams(
            collective_id=1, has_side_effects=True, vmem_limit_bytes=VMEM_LIMIT
        ),
        name="coarse",
    )(
        pooled, lift, jnp.transpose(w_coarse, (1, 0, 2)), decode, joining, cells, spread,
    )


def local(features, w_first, w_second, w_lift, w_coarse, w_decode, w_joining):
    chans, size_x, size_y, depth = features.shape
    beyond, rim = halo(features)
    second, pooled = fine(features, beyond, rim, w_first, w_second)
    up = coarse_level(pooled, w_lift, w_coarse, w_decode, w_joining[:, chans:], size_y)
    return join(second, up, w_joining[:, :chans])


def solution(mesh):
    in_specs = (P(None, "gx", "gy", None), P(), P(), P(), P("gy", None, None), P(), P())
    out_specs = P(None, "gx", "gy", None)
    return jax.shard_map(local, mesh=mesh, in_specs=in_specs, out_specs=out_specs, check_vma=False)
```
